128 devices in a mesh: gy: 8 (over x, y_hi), gx: 16 (over z, y_lo, core).
Axes of the slice: x: 4, y: 4 (y_hi: 2, y_lo: 2; y = y_hi * 2 + y_lo), z: 4, core: 2. Of those that a mesh axis runs over, the one named last changes fastest.
Arguments:
- ensemble: float32 [80, 12, 8, 16, 256], P(None, None, 'gy', 'gx'), may hold values from -6 to 6
- obs_value: float32 [3, 8, 16, 32], P(None, 'gy', 'gx'), may hold values from -8 to 8
- obs_var: float32 [3, 8, 16, 32], P(None, 'gy', 'gx'), may hold values from 0.25 to 4
- obs_cell: int32 [3, 8, 16, 32], P(None, 'gy', 'gx'), may hold values from 0 to 255
- obs_field: int32 [3, 8, 16, 32], P(None, 'gy', 'gx'), may hold values from 0 to 11
- obs_count: int32 [3, 8, 16], P(None, 'gy', 'gx'), may hold values from 1 to 32, as said below
Outputs:
- analysis: float32 [80, 12, 8, 16, 256], P(None, None, 'gy', 'gx')
The draws below stay inside these ranges and needn't reach their ends.
Inputs may be any that keep to these rules, and one draw needn't show every extreme that they name: `obs_count`: in every batch some tile owns exactly 32 observations.
All inputs are finite; a program needn't handle non-finite values.
Results may differ from the reference program's by a relative error of at most 0.0003.
Values sent between devices are 32-bit elements; how exact they have to be, the bound alone decides.
A program may use at most 128 MiB of HBM per device.

```python
import math
import jax
import jax.numpy as jnp
from jax import lax

M = 80
F = 12
TY = 16
TX = 16
CELLS = 256
CAP = 32
BATCHES = 3
LOC = 16
N_GY = 8
N_GX = 16


def draw_obs_count(key, part):
    key = jax.random.fold_in(key, 7)
    first = jax.random.fold_in(key, 1)
    second = jax.random.fold_in(key, 2)
    base = jax.random.randint(first, (BATCHES, N_GY, N_GX), 1, CAP + 1)
    chosen = jax.random.randint(second, (BATCHES,), 0, N_GY * N_GX)
    places = jnp.arange(N_GY * N_GX, dtype=jnp.int32).reshape(N_GY, N_GX)
    full = places[None, :, :] == chosen[:, None, None]
    return jnp.where(full, CAP, base).astype(jnp.int32)


def plant(drawn, stream_key, least, largest):
    longest = drawn.shape.index(max(drawn.shape))
    spots = []
    for shift in (0, 1):
        where = [jax.random.randint(jax.random.fold_in(stream_key, axis), (), 0, length) for axis, length in enumerate(drawn.shape)]
        where[longest] = (where[longest] + shift) % drawn.shape[longest]
        spots.append(tuple(where))
    return drawn.at[spots[0]].set(least).at[spots[1]].set(largest)


def shard_levels(own_key, extent, pieces, low, top_value):
    gain = 1.0
    for dim, parts in pieces:
        heights = jax.random.uniform(jax.random.fold_in(jax.random.fold_in(own_key, 6), dim), (parts,), jnp.float32, low / len(pieces), top_value / len(pieces))
        gain = gain * jnp.repeat(jnp.exp(heights), extent[dim] // parts).reshape((-1,) + (1,) * (len(extent) - 1 - dim))
    return gain


def noise(own_key, dims, scale, most, shards=(), held_as=jnp.bfloat16):
    entries = jax.random.normal(own_key, dims, jnp.float32) * scale
    if len(shards) > 0:
        entries = shard_levels(own_key, dims, shards, -0.22, 0.18) * entries
    return jnp.clip(entries, min=-most, max=most).astype(held_as)


def setup_inputs(seed: int = 0) -> dict:
    splits = jax.random.split(jax.random.key(seed), 7)
    ensemble = noise(splits[0], (M, F, N_GY, N_GX, CELLS), 1.0, 6.0, ((2, 8), (3, 16)), jnp.float32)
    obs_value = noise(splits[1], (BATCHES, N_GY, N_GX, CAP), 1.5, 8.0, ((1, 8), (2, 16)), jnp.float32)
    obs_var = jnp.clip(jnp.exp(math.log(4.0) - 2.7725887 * jax.random.uniform(splits[2], (BATCHES, N_GY, N_GX, CAP), jnp.float32) ** shard_levels(splits[2], (BATCHES, N_GY, N_GX, CAP), ((1, 8), (2, 16)), -0.2, 0.2)), 0.25, 4.0)
    obs_cell = plant(jax.random.randint(splits[3], (BATCHES, N_GY, N_GX, CAP), 0, CELLS), jax.random.fold_in(splits[3], 1), 0, CELLS - 1).astype(jnp.int32)
    obs_field = plant(jax.random.randint(splits[4], (BATCHES, N_GY, N_GX, CAP), 0, F), jax.random.fold_in(splits[4], 1), 0, F - 1).astype(jnp.int32)
    obs_count = draw_obs_count(jax.random.fold_in(splits[6], 71), 0)
    return {"ensemble": ensemble, "obs_value": obs_value, "obs_var": obs_var, "obs_cell": obs_cell, "obs_field": obs_field, "obs_count": obs_count}


def gaspari(ratio):
    safe = jnp.maximum(ratio, 1.0)
    inner = (((-0.25 * ratio + 0.5) * ratio + 0.625) * ratio - 5.0 / 3.0) * ratio * ratio + 1.0
    outer = ((((ratio / 12.0 - 0.5) * ratio + 0.625) * ratio + 5.0 / 3.0) * ratio - 5.0) * ratio + 4.0 - 2.0 / (3.0 * safe)
    return jnp.where(ratio <= 1.0, inner, jnp.where(ratio < 2.0, outer, 0.0 * ratio))

def make_packet(members, cells, fields, count, values, variances):
    width = members.shape[0]
    flat = members.reshape(width, -1)
    flat_index = (fields * CELLS + cells).astype(jnp.int32)
    prior = jnp.take(flat, flat_index, axis=1)
    slots = jnp.arange(cells.shape[0], dtype=jnp.int32)
    live = (slots < count).astype(jnp.float32)
    prior_mean = lax.optimization_barrier(jnp.mean(prior, axis=0))
    perturb = (prior - prior_mean) * live
    innov = (values - prior_mean) * live
    side = jnp.stack([innov, variances * live, live, cells.astype(jnp.float32) * live])
    return jnp.concatenate([perturb, side], axis=0)

def analyse(members, window):
    width = members.shape[0]
    slots = window.shape[-1]
    total = 25 * slots
    mean = lax.optimization_barrier(jnp.mean(members, axis=0))
    pert = members - mean
    obs_pert = jnp.transpose(window[:, :, :width, :], (0, 1, 3, 2)).reshape(total, width)
    side = jnp.transpose(window[:, :, width:, :], (2, 0, 1, 3)).reshape(4, total)
    innov = side[0]
    r_eff = side[1] + 1.0 - side[2]
    cellpos = side[3]
    in_row = jnp.floor(cellpos / TX)
    in_col = cellpos - in_row * TX
    offset = (jnp.arange(5) - 2).astype(jnp.float32)
    blank = jnp.zeros((5, 5, slots), jnp.float32)
    obs_row = (offset[:, None, None] * TY + blank).reshape(total) + in_row
    obs_col = (offset[None, :, None] * TX + blank).reshape(total) + in_col
    cell = jnp.arange(CELLS, dtype=jnp.int32)
    cell_row = (cell // TX).astype(jnp.float32)
    cell_col = (cell % TX).astype(jnp.float32)
    rho_cells = gaspari(jnp.sqrt((cell_row[:, None] - obs_row[None, :]) ** 2 + (cell_col[:, None] - obs_col[None, :]) ** 2) / LOC)
    rho_obs = gaspari(jnp.sqrt((obs_row[:, None] - obs_row[None, :]) ** 2 + (obs_col[:, None] - obs_col[None, :]) ** 2) / LOC)
    scale = 1.0 / (width - 1)
    cov_obs = jnp.dot(obs_pert, obs_pert.T, precision=lax.Precision.HIGHEST) * scale
    system = rho_obs * cov_obs + jnp.diag(r_eff)
    lower = jnp.linalg.cholesky(system)
    weights = jax.scipy.linalg.cho_solve((lower, True), innov)
    middle = jax.scipy.linalg.solve_triangular(lower + jnp.diag(jnp.sqrt(r_eff)), obs_pert, lower=True)
    shaped = jax.scipy.linalg.solve_triangular(lower, middle, lower=True, trans=1)
    combined = jnp.concatenate([weights[:, None], shaped], axis=1)

    def one_field(field_pert):
        cross = jnp.dot(field_pert.T, obs_pert.T, precision=lax.Precision.HIGHEST) * scale
        return jnp.dot(rho_cells * cross, combined, precision=lax.Precision.HIGHEST)
    increments = lax.map(one_field, jnp.transpose(pert, (1, 0, 2)))
    new_mean = mean + increments[:, :, 0]
    new_pert = pert - jnp.transpose(increments[:, :, 1:], (2, 0, 1))
    return new_mean[None] + new_pert

def reference(ensemble, obs_value, obs_var, obs_cell, obs_field, obs_count):
    ntiles = N_GY * N_GX
    tiles = jnp.transpose(ensemble, (2, 3, 0, 1, 4)).reshape(ntiles, M, F, CELLS)
    zero = jnp.zeros((), jnp.int32)
    for batch in range(BATCHES):
        packets = jax.vmap(make_packet)(tiles, obs_cell[batch].reshape(ntiles, CAP), obs_field[batch].reshape(ntiles, CAP), obs_count[batch].reshape(ntiles), obs_value[batch].reshape(ntiles, CAP), obs_var[batch].reshape(ntiles, CAP))
        padded = jnp.pad(packets.reshape(N_GY, N_GX, M + 4, CAP), ((2, 2), (2, 2), (0, 0), (0, 0)))

        def one_tile(item):
            members, place = item
            row = (place // N_GX).astype(jnp.int32)
            col = (place % N_GX).astype(jnp.int32)
            window = lax.dynamic_slice(padded, (row, col, zero, zero), (5, 5, M + 4, CAP))
            return analyse(members, window)
        tiles = lax.map(one_tile, (tiles, jnp.arange(ntiles, dtype=jnp.int32)))
    return jnp.transpose(tiles.reshape(N_GY, N_GX, M, F, CELLS), (2, 3, 0, 1, 4))
```

```python
import functools
import jax
import jax.numpy as jnp
from jax import lax
from jax.experimental import pallas as pl
from jax.experimental.pallas import tpu as pltpu
from jax.sharding import PartitionSpec as P

M = 80
F = 12
TX = 16
TY = 16
CELLS = 256
CAP = 32
LOC = 16
BATCHES = 3
N_GY = 8
N_GX = 16
SLOTS = 25 * CAP
NB = 128
BLOCKS = 7
WIDE = NB * BLOCKS
COLS = F * CELLS
HI = lax.Precision.HIGHEST
MESH = pl.DeviceIdType.MESH
REACH = (-2, -1, 1, 2)
F32 = jnp.float32
BF = jnp.bfloat16


def gaspari(ratio):
    safe = jnp.maximum(ratio, 1.0)
    inner = (((-0.25 * ratio + 0.5) * ratio + 0.625) * ratio - 5.0 / 3.0) * ratio * ratio + 1.0
    outer = (
        ((((ratio / 12.0 - 0.5) * ratio + 0.625) * ratio + 5.0 / 3.0) * ratio - 5.0) * ratio
        + 4.0
        - (2.0 / 3.0) / safe
    )
    return jnp.where(ratio <= 1.0, inner, jnp.where(ratio < 2.0, outer, 0.0))


def taper(row_a, col_a, row_b, col_b):
    square = (row_a - row_b) ** 2 + (col_a - col_b) ** 2
    return gaspari(jnp.sqrt(square) * (1.0 / LOC))


def split3(value):
    high = value.astype(BF)
    rest = value - high.astype(F32)
    mid = rest.astype(BF)
    low = (rest - mid.astype(F32)).astype(BF)
    return high, mid, low


def split2(value):
    high = value.astype(BF)
    return high, (value - high.astype(F32)).astype(BF)


def dot_nn(a, b, precision=None):
    return lax.dot_general(a, b, (((1,), (0,)), ((), ())), precision=precision, preferred_element_type=F32)


def dot_nt(a, b, precision=None):
    return lax.dot_general(a, b, (((1,), (1,)), ((), ())), precision=precision, preferred_element_type=F32)


def dot_tn(a, b, precision=None):
    return lax.dot_general(a, b, (((0,), (0,)), ((), ())), precision=precision, preferred_element_type=F32)


def eliminate(chain, root):
    lane = lax.broadcasted_iota(jnp.int32, (8, NB), 1)
    row = lax.broadcasted_iota(jnp.int32, (8, NB), 0)
    member = lane < M
    for k in range(8):
        base = 16 * k
        sect = [[chain[base + 8 * h : base + 8 * h + 8, NB * s : NB * s + NB] for h in range(2)] for s in range(3)]
        dev = [jnp.broadcast_to(root[base + 8 * h : base + 8 * h + 8, :], (8, NB)) for h in range(2)]
        bc = [
            [jnp.broadcast_to(sect[0][h][:, base + i : base + i + 1], (8, NB)) for h in range(2)]
            for i in range(16)
        ]
        piv = [jnp.ones((8, NB), F32), jnp.ones((8, NB), F32)]
        for j in range(16):
            hj, rj = divmod(j, 8)
            piv[hj] = jnp.where(row == rj, bc[j][hj], piv[hj])
            pivot = jnp.broadcast_to(bc[j][hj][rj : rj + 1, :], (8, NB))
            inv = 1.0 / pivot
            rs = lax.rsqrt(pivot)
            droot = jnp.broadcast_to(dev[hj][rj : rj + 1, :], (8, NB))
            scale_y = jnp.where(member, rs / (pivot * rs + droot), inv)
            for h in range(hj, 2):
                column = bc[j][h]
                if h == hj:
                    if rj == 7:
                        continue
                    column = jnp.where(row > rj, column, 0.0)
                mult = column * inv
                mult_y = column * scale_y
                for i in range(j + 1, 16):
                    bc[i][h] = bc[i][h] - mult * jnp.broadcast_to(bc[i][hj][rj : rj + 1, :], (8, NB))
                sect[0][h] = sect[0][h] - mult * jnp.broadcast_to(sect[0][hj][rj : rj + 1, :], (8, NB))
                sect[1][h] = sect[1][h] - mult * jnp.broadcast_to(sect[1][hj][rj : rj + 1, :], (8, NB))
                sect[2][h] = sect[2][h] - mult_y * jnp.broadcast_to(sect[2][hj][rj : rj + 1, :], (8, NB))
        for h in range(2):
            rs = lax.rsqrt(piv[h])
            sect[0][h] = sect[0][h] * rs
            sect[1][h] = sect[1][h] * rs
            sect[2][h] = sect[2][h] * jnp.where(member, 1.0 / (piv[h] * rs + dev[h]), rs)
            for s in range(1, 3):
                chain[base + 8 * h : base + 8 * h + 8, NB * s : NB * s + NB] = sect[s][h]
        if k < 7:
            parts = [split3(jnp.concatenate(sect[s], axis=0)) for s in range(3)]
            high, mid, low = [jnp.concatenate([parts[s][p] for s in range(3)], axis=1) for p in range(3)]
            uh, um, ul = parts[0]
            left = jnp.concatenate([uh, uh, um, uh, ul, um], axis=0)
            right = jnp.concatenate([high, mid, high, low, high, mid], axis=0)
            update = dot_tn(left, right)
            chain[base + 16 :, :] = chain[base + 16 :, :] - update[base + 16 :, :]


def write_packet(members, obs, packet_ref):
    index = obs[:, 0:1].astype(jnp.int32)
    live = obs[:, 3:4]
    hot = (lax.broadcasted_iota(jnp.int32, (CAP, COLS), 1) == index).astype(F32).astype(BF)
    got = dot_nt(hot, jnp.concatenate(split3(members), axis=0))
    prior = got[:, 0:M] + got[:, M : 2 * M] + got[:, 2 * M :]
    mean = jnp.sum(prior, axis=1, keepdims=True) * (1.0 / M)
    perturb = jnp.concatenate([(prior - mean) * live, jnp.zeros((CAP, NB - M), F32)], axis=1)
    cell = obs[:, 4:5]
    in_row = jnp.floor(cell * (1.0 / TX))
    lane = lax.broadcasted_iota(jnp.int32, (CAP, NB), 1)
    sides = ((obs[:, 1:2] - mean) * live, obs[:, 2:3] * live, live, cell * live, in_row, cell - in_row * TX)
    for place, side in enumerate(sides):
        perturb = jnp.where(lane == M + place, side, perturb)
    packet_ref[...] = perturb


def packet_kernel(mem_ref, obs_ref, packet_ref):
    write_packet(mem_ref[...], obs_ref[0], packet_ref)


def exchange_kernel(packet_ref, win_ref, send_sem, recv_sem):
    gy = lax.axis_index("gy")
    gx = lax.axis_index("gx")
    row_of = [lax.rem(gy + step + N_GY, N_GY) for step in REACH]
    col_of = [lax.rem(gx + step + N_GX, N_GX) for step in REACH]
    barrier = pltpu.get_barrier_semaphore()
    for col in col_of:
        pl.semaphore_signal(barrier, inc=1, device_id=(gy, col), device_id_type=MESH)
    for row in row_of:
        pl.semaphore_signal(barrier, inc=1, device_id=(row, gx), device_id_type=MESH)
    win_ref[2, 2] = packet_ref[...]
    pl.semaphore_wait(barrier, 8)
    across = []
    for i, step in enumerate(REACH):
        copy = pltpu.make_async_remote_copy(
            src_ref=packet_ref,
            dst_ref=win_ref.at[2, 2 - step],
            send_sem=send_sem.at[i],
            recv_sem=recv_sem.at[i],
            device_id=(gy, col_of[i]),
            device_id_type=MESH,
        )
        copy.start()
        across.append(copy)
    for copy in across:
        copy.wait_recv()
    along = []
    for i, step in enumerate(REACH):
        copy = pltpu.make_async_remote_copy(
            src_ref=win_ref.at[2],
            dst_ref=win_ref.at[2 - step],
            send_sem=send_sem.at[4 + i],
            recv_sem=recv_sem.at[4 + i],
            device_id=(row_of[i], gx),
            device_id_type=MESH,
        )
        copy.start()
        along.append(copy)
    for copy in across:
        copy.wait_send()
    for copy in along:
        copy.wait()


def analysis_kernel(spot, win_ref, mem_ref, *rest, last):
    if last:
        out_ref, *scratch = rest
    else:
        obs_ref, out_ref, packet_ref, *scratch = rest
    mat, ycomp, ypack, xpack, chain, root, linv, solt, acc, rho = scratch
    scale = 1.0 / (M - 1)

    tile = lax.broadcasted_iota(jnp.int32, (32, 1), 0)
    tile_row = spot[0] + tile // 5 - 2
    tile_col = spot[1] + tile % 5 - 2
    inside = (tile_row >= 0) & (tile_row < N_GY) & (tile_col >= 0) & (tile_col < N_GX) & (tile < 25)
    counts = jnp.concatenate(
        [jnp.sum(win_ref[CAP * t : CAP * t + CAP, :], axis=0, keepdims=True) for t in range(25)]
        + [jnp.zeros((7, NB), F32)],
        axis=0,
    )[:, M + 2 : M + 3]
    counts = jnp.where(inside, counts, 0.0)
    n = jnp.sum(counts).astype(jnp.int32)
    nb = (n + NB - 1) // NB
    slot_lane = lax.broadcasted_iota(jnp.int32, (1, SLOTS), 1)
    slot_tile = slot_lane // CAP
    slot_k = (slot_lane % CAP).astype(F32)
    base = jnp.sum(jnp.where(tile < slot_tile, counts, 0.0), axis=0, keepdims=True)
    own = jnp.sum(jnp.where(tile == slot_tile, counts, 0.0), axis=0, keepdims=True)
    place = jnp.where(slot_k < own, base + slot_k, -1.0).astype(jnp.int32)

    mem = mem_ref[...]
    mean = jnp.sum(mem, axis=0, keepdims=True) * (1.0 / M)
    xh, xl = split2(mem - mean)
    xpack[0:M, :] = xh
    xpack[M : 2 * M, :] = xh
    xpack[2 * M : 3 * M, :] = xl
    xpack[3 * M :, :] = jnp.zeros((256 - 3 * M, COLS), BF)

    slot = lax.broadcasted_iota(jnp.int32, (SLOTS, NB), 0) // CAP
    slane = lax.broadcasted_iota(jnp.int32, (SLOTS, NB), 1)
    shift = jnp.where(slane == M + 4, (slot // 5 - 2) * TY, jnp.where(slane == M + 5, (slot % 5 - 2) * TX, 0))
    win = win_ref[...] + shift.astype(F32)
    win3 = jnp.concatenate(split3(win), axis=1)
    mat[...] = jnp.zeros_like(mat)
    ycomp[...] = jnp.zeros_like(ycomp)
    solt[...] = jnp.zeros_like(solt)
    acc[...] = jnp.zeros_like(acc)
    lane = lax.broadcasted_iota(jnp.int32, (NB, NB), 1)

    @pl.loop(0, nb)
    def _(b):
        at = pl.ds(pl.multiple_of(b * NB, NB), NB)
        target = lax.broadcasted_iota(jnp.int32, (NB, SLOTS), 0) + b * NB
        hot = (target == place).astype(F32).astype(BF)
        got = dot_nn(hot, win3)
        full = got[:, 0:NB] + got[:, NB : 2 * NB] + got[:, 2 * NB :]
        ycomp[at, :] = full
        y = jnp.where(lane < M, full, 0.0)
        high = y.astype(BF).astype(F32)
        turned = pltpu.roll(y - high, M, 1)
        ypack[at, 0:NB] = jnp.where(lane < M, high, turned).astype(BF)
        ypack[at, NB:] = jnp.where(lane < 2 * M - NB, turned, pltpu.roll(high, 2 * M - NB, 1)).astype(BF)

    lane_w = lax.broadcasted_iota(jnp.int32, (WIDE, NB), 1)
    yall = jnp.where(lane_w < M, ycomp[...], 0.0)
    side = jnp.concatenate(
        [jnp.transpose(ycomp[NB * b : NB * b + NB, :])[80:88, :] for b in range(BLOCKS)], axis=1
    )
    row_b, col_b = side[4:5, :], side[5:6, :]
    cell = lax.broadcasted_iota(jnp.int32, (1, CELLS), 1)
    cell_row = (cell // TX).astype(F32)
    cell_col = (cell % TX).astype(F32)
    srow = lax.broadcasted_iota(jnp.int32, (NB, NB), 0)
    wide_lane = lax.broadcasted_iota(jnp.int32, (NB, WIDE), 1)
    wide_row = lax.broadcasted_iota(jnp.int32, (NB, WIDE), 0)

    @pl.loop(0, nb)
    def _(b):
        at = pl.ds(pl.multiple_of(b * NB, NB), NB)
        yc = ycomp[at, :]
        r_eff = yc[:, 81:82] + 1.0 - yc[:, 82:83]
        row_a, col_a = yc[:, 84:85], yc[:, 85:86]
        gram = dot_nt(jnp.where(lane < M, yc, 0.0), yall, HI) * scale
        system = taper(row_a, col_a, row_b, col_b) * gram
        mat[at, 0:WIDE] = system + jnp.where(wide_lane == wide_row + b * NB, r_eff, 0.0)
        mat[at, WIDE:] = jnp.where(lane <= M, yc, 0.0)
        rho[at, :] = taper(row_a, col_a, cell_row, cell_col) * scale
        root[...] = jnp.broadcast_to(jnp.sqrt(r_eff), (NB, NB))

        for k in range(1, BLOCKS):

            @pl.when(b == k)
            def _():
                top = slice(0, NB * k)
                here = slice(NB * k, NB * k + NB)
                update = dot_tn(mat[top, here], mat[top, NB * k :], HI)
                mat[here, NB * k :] = mat[here, NB * k :] - update

        for k in range(BLOCKS):

            @pl.when(b == k)
            def _():
                chain[:, 0:NB] = mat[NB * k : NB * k + NB, NB * k : NB * k + NB]

        chain[:, NB : 2 * NB] = jnp.where(lane == srow, 1.0, 0.0)
        chain[:, 2 * NB :] = mat[at, WIDE:]
        eliminate(chain, root)
        inverse = chain[:, NB : 2 * NB]
        linv[at, :] = inverse
        mat[at, WIDE:] = chain[:, 2 * NB :]

        for k in range(BLOCKS - 1):

            @pl.when(b == k)
            def _():
                here = slice(NB * k, NB * k + NB)
                right = slice(NB * k + NB, WIDE)
                mat[here, right] = dot_nn(inverse, mat[here, right], HI)

    for k in range(BLOCKS - 1, -1, -1):

        @pl.when(k < nb)
        def _():
            here = slice(NB * k, NB * k + NB)
            target = jnp.transpose(mat[here, WIDE:])
            if k < BLOCKS - 1:
                right = slice(NB * k + NB, WIDE)
                target = target - dot_nt(solt[:, right], mat[here, right], HI)
            solt[:, here] = dot_nn(target, linv[here, :], HI)

    for k in range(BLOCKS):

        @pl.when(k < nb)
        def _():
            here = slice(NB * k, NB * k + NB)
            zh, zl = split2(solt[0:96, here])
            left = jnp.concatenate(
                [jnp.concatenate([zh, zh], axis=1), jnp.concatenate([zl, jnp.zeros_like(zl)], axis=1)], axis=0
            )
            taps = rho[here, :]
            yb = ypack[here, :]

            @pl.loop(0, F)
            def _(f):
                at = pl.ds(pl.multiple_of(f * CELLS, CELLS), CELLS)
                cross = dot_nn(yb, xpack[:, at]) * taps
                gh, gl = split2(cross)
                both = dot_nn(left, jnp.concatenate([gh, gl], axis=0))
                acc[:, at] = acc[:, at] + both[0:96] + both[96:]

    new = mem_ref[...] + acc[M : M + 1, :] - acc[0:M, :]
    out_ref[...] = new
    if not last:
        write_packet(new, obs_ref[0], packet_ref)


VM = pl.BlockSpec(memory_space=pltpu.VMEM)
SM = pl.BlockSpec(memory_space=pltpu.SMEM)
PACKET = jax.ShapeDtypeStruct((CAP, NB), F32)
STATE = jax.ShapeDtypeStruct((M, COLS), F32)


def first_packet(members, obs):
    return pl.pallas_call(
        packet_kernel,
        out_shape=PACKET,
        in_specs=[VM, VM],
        out_specs=VM,
        compiler_params=pltpu.CompilerParams(vmem_limit_bytes=32 * 1024 * 1024),
    )(members, obs)


def exchange(packet):
    return pl.pallas_call(
        exchange_kernel,
        out_shape=jax.ShapeDtypeStruct((5, 5, CAP, NB), F32),
        in_specs=[VM],
        out_specs=VM,
        scratch_shapes=[pltpu.SemaphoreType.DMA((8,)), pltpu.SemaphoreType.DMA((8,))],
        compiler_params=pltpu.CompilerParams(collective_id=0, has_side_effects=True),
    )(packet)


def analyse(spot, window, members, obs):
    last = obs is None
    return pl.pallas_call(
        functools.partial(analysis_kernel, last=last),
        out_shape=STATE if last else (STATE, PACKET),
        in_specs=[SM, VM, VM] + ([] if last else [VM]),
        out_specs=VM if last else (VM, VM),
        scratch_shapes=[
            pltpu.VMEM((WIDE, WIDE + NB), F32),
            pltpu.VMEM((WIDE, NB), F32),
            pltpu.VMEM((WIDE, 256), BF),
            pltpu.VMEM((256, COLS), BF),
            pltpu.VMEM((NB, 3 * NB), F32),
            pltpu.VMEM((NB, NB), F32),
            pltpu.VMEM((WIDE, NB), F32),
            pltpu.VMEM((NB, WIDE), F32),
            pltpu.VMEM((96, COLS), F32),
            pltpu.VMEM((WIDE, CELLS), F32),
        ],
        compiler_params=pltpu.CompilerParams(vmem_limit_bytes=48 * 1024 * 1024),
    )(spot, window, members, *([] if last else [obs]))


def gather_obs(obs_value, obs_var, obs_cell, obs_field, obs_count):
    index = obs_field * CELLS + obs_cell
    live = jnp.arange(CAP, dtype=jnp.int32) < obs_count[:, None]
    columns = [index.astype(F32), obs_value, obs_var, live.astype(F32), obs_cell.astype(F32)]
    return jnp.stack(columns + [jnp.zeros_like(obs_value)] * 3, axis=-1)


def per_device(ensemble, obs_value, obs_var, obs_cell, obs_field, obs_count):
    members = ensemble.reshape(M, COLS)
    obs = gather_obs(
        obs_value[:, 0, 0], obs_var[:, 0, 0], obs_cell[:, 0, 0], obs_field[:, 0, 0], obs_count[:, 0, 0]
    )
    spot = jnp.stack([lax.axis_index("gy"), lax.axis_index("gx")]).astype(jnp.int32)
    packet = first_packet(members, obs[0:1])
    for batch in range(BATCHES):
        window = exchange(packet).reshape(SLOTS, NB)
        if batch < BATCHES - 1:
            members, packet = analyse(spot, window, members, obs[batch + 1 : batch + 2])
        else:
            members = analyse(spot, window, members, None)
    return members.reshape(ensemble.shape)


def solution(mesh):
    return jax.shard_map(
        per_device,
        mesh=mesh,
        in_specs=(
            P(None, None, "gy", "gx", None),
            P(None, "gy", "gx", None),
            P(None, "gy", "gx", None),
            P(None, "gy", "gx", None),
            P(None, "gy", "gx", None),
            P(None, "gy", "gx"),
        ),
        out_specs=P(None, None, "gy", "gx", None),
        check_vma=False,
    )
```

```python
import functools
import jax
import jax.numpy as jnp
from jax import lax
from jax.experimental import pallas as pl
from jax.experimental.pallas import tpu as pltpu
from jax.sharding import PartitionSpec as P

M = 80
F = 12
TX = 16
TY = 16
CELLS = 256
CAP = 32
LOC = 16
BATCHES = 3
N_GY = 8
N_GX = 16
SLOTS = 25 * CAP
NB = 128
BLOCKS = 7
WIDE = NB * BLOCKS
COLS = F * CELLS
PARTS = COLS // NB
UNROLL = 4
STEP = 16
MESH = pl.DeviceIdType.MESH
F32 = jnp.float32
BF = jnp.bfloat16


def taper(row_a, col_a, row_b, col_b):
    down, over = row_a - row_b, col_a - col_b
    square = down * down + over * over
    inverse = lax.rsqrt(jnp.maximum(square, 1e-20))
    ratio = square * inverse * (1.0 / LOC)
    inner = (((-0.25 * ratio + 0.5) * ratio + 0.625) * ratio - 5.0 / 3.0) * ratio * ratio + 1.0
    outer = (
        ((((ratio * (1.0 / 12.0) - 0.5) * ratio + 0.625) * ratio + 5.0 / 3.0) * ratio - 5.0) * ratio
        + 4.0
        - (2.0 / 3.0 * LOC) * inverse
    )
    return jnp.where(ratio <= 1.0, inner, jnp.where(ratio < 2.0, outer, 0.0))


def split3(value):
    high = value.astype(BF)
    rest = value - high.astype(F32)
    mid = rest.astype(BF)
    low = (rest - mid.astype(F32)).astype(BF)
    return high, mid, low


def split2(value):
    high = value.astype(BF)
    return high, (value - high.astype(F32)).astype(BF)


def dot_nn(a, b, precision=None):
    return lax.dot_general(a, b, (((1,), (0,)), ((), ())), precision=precision, preferred_element_type=F32)


def dot_nt(a, b, precision=None):
    return lax.dot_general(a, b, (((1,), (1,)), ((), ())), precision=precision, preferred_element_type=F32)


def dot_tn(a, b, precision=None):
    return lax.dot_general(a, b, (((0,), (0,)), ((), ())), precision=precision, preferred_element_type=F32)


def three(dot, a, b):
    return dot(a[0], b[0]) + dot(a[1], b[0]) + dot(a[0], b[1])


def eliminate(chain, root, rows):
    lane = lax.broadcasted_iota(jnp.int32, (8, NB), 1)
    row = lax.broadcasted_iota(jnp.int32, (8, NB), 0)
    member = lane < M
    halves = STEP // 8
    for k in range(NB // STEP):

        @pl.when(rows > STEP * k)
        def _():
            base = STEP * k
            sect = [[chain[base + 8 * h : base + 8 * h + 8, NB * s : NB * s + NB] for h in range(halves)] for s in range(3)]
            dev = [jnp.broadcast_to(root[base + 8 * h : base + 8 * h + 8, :], (8, NB)) for h in range(halves)]
            bc = [
                [jnp.broadcast_to(sect[0][h][:, base + i : base + i + 1], (8, NB)) for h in range(halves)]
                for i in range(STEP)
            ]
            piv = [jnp.ones((8, NB), F32) for h in range(halves)]
            for j in range(STEP):
                hj, rj = divmod(j, 8)
                piv[hj] = jnp.where(row == rj, bc[j][hj], piv[hj])
                pivot = jnp.broadcast_to(bc[j][hj][rj : rj + 1, :], (8, NB))
                inv = 1.0 / pivot
                rs = lax.rsqrt(pivot)
                droot = jnp.broadcast_to(dev[hj][rj : rj + 1, :], (8, NB))
                scale_y = jnp.where(member, rs / (pivot * rs + droot), inv)
                for h in range(hj, halves):
                    column = bc[j][h]
                    if h == hj:
                        if rj == 7:
                            continue
                        column = jnp.where(row > rj, column, 0.0)
                    mult = column * inv
                    mult_y = column * scale_y
                    for i in range(j + 1, STEP):
                        bc[i][h] = bc[i][h] - mult * jnp.broadcast_to(bc[i][hj][rj : rj + 1, :], (8, NB))
                    sect[0][h] = sect[0][h] - mult * jnp.broadcast_to(sect[0][hj][rj : rj + 1, :], (8, NB))
                    sect[1][h] = sect[1][h] - mult * jnp.broadcast_to(sect[1][hj][rj : rj + 1, :], (8, NB))
                    sect[2][h] = sect[2][h] - mult_y * jnp.broadcast_to(sect[2][hj][rj : rj + 1, :], (8, NB))
            for h in range(halves):
                rs = lax.rsqrt(piv[h])
                sect[0][h] = sect[0][h] * rs
                sect[1][h] = sect[1][h] * rs
                sect[2][h] = sect[2][h] * jnp.where(member, 1.0 / (piv[h] * rs + dev[h]), rs)
                for s in range(1, 3):
                    chain[base + 8 * h : base + 8 * h + 8, NB * s : NB * s + NB] = sect[s][h]
            if k < NB // STEP - 1:
                parts = [split3(jnp.concatenate(sect[s], axis=0)) for s in range(3)]
                high, mid, low = [jnp.concatenate([parts[s][p] for s in range(3)], axis=1) for p in range(3)]
                uh, um, ul = parts[0]
                left = jnp.concatenate([uh, uh, um, uh, ul, um], axis=0)
                right = jnp.concatenate([high, mid, high, low, high, mid], axis=0)
                update = dot_tn(left, right)
                chain[base + STEP :, :] = chain[base + STEP :, :] - update[base + STEP :, :]


def write_packet(members, obs, packet_ref):
    index = obs[:, 0:1].astype(jnp.int32)
    live = obs[:, 3:4]
    hot = (lax.broadcasted_iota(jnp.int32, (CAP, COLS), 1) == index).astype(F32).astype(BF)
    got = dot_nt(hot, jnp.concatenate(split3(members), axis=0))
    prior = got[:, 0:M] + got[:, M : 2 * M] + got[:, 2 * M :]
    mean = jnp.sum(prior, axis=1, keepdims=True) * (1.0 / M)
    perturb = jnp.concatenate([(prior - mean) * live, jnp.zeros((CAP, NB - M), F32)], axis=1)
    cell = obs[:, 4:5]
    in_row = jnp.floor(cell * (1.0 / TX))
    lane = lax.broadcasted_iota(jnp.int32, (CAP, NB), 1)
    sides = ((obs[:, 1:2] - mean) * live, obs[:, 2:3] * live, live, cell * live, in_row, cell - in_row * TX)
    for place, side in enumerate(sides):
        perturb = jnp.where(lane == M + place, side, perturb)
    packet_ref[...] = perturb


def packet_kernel(rows_ref, obs_ref, mem_ref, packet_ref):
    for part in range(PARTS):
        mem_ref[:, NB * part : NB * part + NB] = rows_ref[pl.ds(part, M, stride=PARTS), :]
    write_packet(mem_ref[...], obs_ref[0], packet_ref)


def exchange_kernel(packet_ref, win_ref, send_sem, recv_sem):
    gy = lax.axis_index("gy")
    gx = lax.axis_index("gx")
    reach = range(-2, 3)
    row_of = {step: lax.rem(gy + step + N_GY, N_GY) for step in reach}
    col_of = {step: lax.rem(gx + step + N_GX, N_GX) for step in reach}
    others = [(down, over) for down in reach for over in reach if (down, over) != (0, 0)]
    barrier = pltpu.get_barrier_semaphore()
    for down, over in others:
        pl.semaphore_signal(barrier, inc=1, device_id=(row_of[down], col_of[over]), device_id_type=MESH)
    win_ref[2, 2] = packet_ref[...]
    pl.semaphore_wait(barrier, len(others))
    copies = []
    for place, (down, over) in enumerate(others):
        copy = pltpu.make_async_remote_copy(
            src_ref=packet_ref,
            dst_ref=win_ref.at[2 - down, 2 - over],
            send_sem=send_sem.at[place],
            recv_sem=recv_sem.at[place],
            device_id=(row_of[down], col_of[over]),
            device_id_type=MESH,
        )
        copy.start()
        copies.append(copy)
    for copy in copies:
        copy.wait()


def analysis_kernel(spot, win_ref, mem_ref, *rest, batch):
    last = batch == BATCHES - 1
    if last:
        out_ref, *scratch = rest
    else:
        obs_ref, out_ref, packet_ref, *scratch = rest
    uh, ul, side_sys, sols, ycomp, ypack, yturn, xpack, chain, root, vh, vl, zth, ztl, rho = scratch
    scale = 1.0 / (M - 1)

    tile = lax.broadcasted_iota(jnp.int32, (32, 1), 0)
    tile_row = spot[0] + tile // 5 - 2
    tile_col = spot[1] + tile % 5 - 2
    inside = (tile_row >= 0) & (tile_row < N_GY) & (tile_col >= 0) & (tile_col < N_GX) & (tile < 25)
    counts = jnp.concatenate(
        [jnp.sum(win_ref[CAP * t : CAP * t + CAP, :], axis=0, keepdims=True) for t in range(25)]
        + [jnp.zeros((7, NB), F32)],
        axis=0,
    )[:, M + 2 : M + 3]
    counts = jnp.where(inside, counts, 0.0)
    n = jnp.sum(counts).astype(jnp.int32)
    nb = (n + NB - 1) // NB
    slot_lane = lax.broadcasted_iota(jnp.int32, (1, SLOTS), 1)
    slot_tile = slot_lane // CAP
    slot_k = (slot_lane % CAP).astype(F32)
    base = jnp.sum(jnp.where(tile < slot_tile, counts, 0.0), axis=0, keepdims=True)
    own = jnp.sum(jnp.where(tile == slot_tile, counts, 0.0), axis=0, keepdims=True)
    place = jnp.where(slot_k < own, base + slot_k, -1.0).astype(jnp.int32)

    mem = mem_ref[...]
    mean = jnp.sum(mem, axis=0, keepdims=True) * (1.0 / M)
    xh, xl = split2(mem - mean)
    xpack[0:M, :] = xh
    xpack[M : 2 * M, :] = xh
    xpack[2 * M : 3 * M, :] = xl
    xpack[3 * M :, :] = jnp.zeros((256 - 3 * M, COLS), BF)

    slot = lax.broadcasted_iota(jnp.int32, (SLOTS, NB), 0) // CAP
    slane = lax.broadcasted_iota(jnp.int32, (SLOTS, NB), 1)
    shift = jnp.where(slane == M + 4, (slot // 5 - 2) * TY, jnp.where(slane == M + 5, (slot % 5 - 2) * TX, 0))
    win = win_ref[...] + shift.astype(F32)
    win2 = jnp.concatenate(split2(win), axis=1)
    ycomp[...] = jnp.zeros_like(ycomp)
    yturn[...] = jnp.zeros_like(yturn)
    zth[...] = jnp.zeros_like(zth)
    ztl[...] = jnp.zeros_like(ztl)
    lane = lax.broadcasted_iota(jnp.int32, (NB, NB), 1)

    @pl.loop(0, nb)
    def _(b):
        at = pl.ds(pl.multiple_of(b * NB, NB), NB)
        target = lax.broadcasted_iota(jnp.int32, (NB, SLOTS), 0) + b * NB
        hot = (target == place).astype(F32).astype(BF)
        got = dot_nn(hot, win2)
        high, low = got[:, 0:NB], got[:, NB:]
        ycomp[at, :] = high + low
        high = jnp.where(lane < M, high, 0.0)
        low = jnp.where(lane < M, low, 0.0)
        turned = pltpu.roll(low, M, 1)
        ypack[at, 0:NB] = jnp.where(lane < M, high, turned).astype(BF)
        ypack[at, NB:] = jnp.where(lane < 2 * M - NB, turned, pltpu.roll(high, 2 * M - NB, 1)).astype(BF)
        turned = pltpu.roll(high, M, 1)
        yturn[at, 0:NB] = jnp.where(lane < M, high, turned).astype(BF)
        yturn[at, NB:] = jnp.where(lane < 2 * M - NB, turned, pltpu.roll(low, 2 * M - NB, 1)).astype(BF)

    side = jnp.concatenate(
        [jnp.transpose(ycomp[NB * b : NB * b + NB, :])[80:88, :] for b in range(BLOCKS)], axis=1
    )
    row_b, col_b = side[4:5, :], side[5:6, :]
    cell = lax.broadcasted_iota(jnp.int32, (1, CELLS), 1)
    cell_row = (cell // TX).astype(F32)
    cell_col = (cell % TX).astype(F32)
    srow = lax.broadcasted_iota(jnp.int32, (NB, NB), 0)

    @pl.loop(0, nb)
    def _(b):
        at = pl.ds(pl.multiple_of(b * NB, NB), NB)
        yc = ycomp[at, :]
        r_eff = yc[:, 81:82] + 1.0 - yc[:, 82:83]
        row_a, col_a = yc[:, 84:85], yc[:, 85:86]
        rho[at, :] = taper(row_a, col_a, cell_row, cell_col) * scale
        root[...] = jnp.broadcast_to(jnp.sqrt(r_eff), (NB, NB))
        left = ypack[at, :]

        for k in range(BLOCKS):

            @pl.when(b == k)
            def _():
                top = slice(0, NB * k)
                here = slice(NB * k, NB * k + NB)
                gram = dot_nt(left, yturn[NB * k :, :]) * scale
                system = taper(row_a, col_a, row_b[:, NB * k :], col_b[:, NB * k :]) * gram
                sides = jnp.where(lane <= M, yc, 0.0)
                if k:
                    update = three(dot_tn, (uh[top, here], ul[top, here]), (uh[top, NB * k :], ul[top, NB * k :]))
                    system = system - update[:, : WIDE - NB * k]
                    sides = sides - update[:, WIDE - NB * k :]
                chain[:, 0:NB] = system[:, 0:NB] + jnp.where(lane == srow, r_eff, 0.0)
                chain[:, 2 * NB :] = sides
                if k < BLOCKS - 1:
                    side_sys[:, NB * k + NB :] = system[:, NB:]

        chain[:, NB : 2 * NB] = jnp.where(lane == srow, 1.0, 0.0)
        eliminate(chain, root, n - b * NB)
        inverse = split2(chain[:, NB : 2 * NB])
        vh[at, :], vl[at, :] = inverse
        solved = chain[:, 2 * NB :]
        sols[at, :] = solved
        uh[at, WIDE:], ul[at, WIDE:] = split2(solved)

        for k in range(BLOCKS - 1):

            @pl.when(b == k)
            def _():
                here = slice(NB * k, NB * k + NB)
                right = slice(NB * k + NB, WIDE)
                uh[here, right], ul[here, right] = split2(three(dot_nn, inverse, split2(side_sys[:, right])))

    for k in range(BLOCKS - 1, -1, -1):

        @pl.when(k < nb)
        def _():
            here = slice(NB * k, NB * k + NB)
            target = jnp.transpose(sols[here, :])
            if k < BLOCKS - 1:
                right = slice(NB * k + NB, WIDE)
                target = target - three(dot_nt, (zth[:, right], ztl[:, right]), (uh[here, right], ul[here, right]))
            zth[:, here], ztl[:, here] = split2(three(dot_nn, split2(target), (vh[here, :], vl[here, :])))

    for used in range(1, BLOCKS + 1):

        @pl.when(nb == used)
        def _():
            here = slice(0, NB * used)
            zh = zth[0:96, here]
            both = jnp.concatenate([zh, ztl[0:96, here]], axis=0)

            def one_field(f, carry):
                at = pl.ds(pl.multiple_of(f * CELLS, CELLS), CELLS)
                gh, gl = split2(dot_nn(ypack[here, :], xpack[:, at]) * rho[here, :])
                part = dot_nn(both, gh)
                gain = part[0:96] + part[96:] + dot_nn(zh, gl)
                new = mem_ref[:, at] + gain[M : M + 1, :] - gain[0:M, :]
                if last:
                    out_ref[pl.ds(2 * f, M, stride=PARTS), :] = new[:, 0:NB]
                    out_ref[pl.ds(2 * f + 1, M, stride=PARTS), :] = new[:, NB:]
                else:
                    out_ref[:, at] = new
                return carry

            lax.fori_loop(0, F, one_field, 0, unroll=UNROLL)

    if not last:
        write_packet(out_ref[...], obs_ref[batch + 1], packet_ref)


VM = pl.BlockSpec(memory_space=pltpu.VMEM)
SM = pl.BlockSpec(memory_space=pltpu.SMEM)
PACKET = jax.ShapeDtypeStruct((CAP, NB), F32)
STATE = jax.ShapeDtypeStruct((M, COLS), F32)
ROWS = jax.ShapeDtypeStruct((M * PARTS, NB), F32)


def first_packet(rows, obs):
    return pl.pallas_call(
        packet_kernel,
        out_shape=(STATE, PACKET),
        in_specs=[VM, VM],
        out_specs=(VM, VM),
        compiler_params=pltpu.CompilerParams(vmem_limit_bytes=32 * 1024 * 1024),
    )(rows, obs)


def exchange(packet):
    return pl.pallas_call(
        exchange_kernel,
        out_shape=jax.ShapeDtypeStruct((5, 5, CAP, NB), F32),
        in_specs=[VM],
        out_specs=VM,
        scratch_shapes=[pltpu.SemaphoreType.DMA((24,)), pltpu.SemaphoreType.DMA((24,))],
        compiler_params=pltpu.CompilerParams(collective_id=0, has_side_effects=True),
    )(packet)


def analyse(spot, window, members, obs, batch):
    last = batch == BATCHES - 1
    return pl.pallas_call(
        functools.partial(analysis_kernel, batch=batch),
        out_shape=ROWS if last else (STATE, PACKET),
        in_specs=[SM, VM, VM] + ([] if last else [VM]),
        out_specs=VM if last else (VM, VM),
        scratch_shapes=[
            pltpu.VMEM((WIDE, WIDE + NB), BF),
            pltpu.VMEM((WIDE, WIDE + NB), BF),
            pltpu.VMEM((NB, WIDE), F32),
            pltpu.VMEM((WIDE, NB), F32),
            pltpu.VMEM((WIDE, NB), F32),
            pltpu.VMEM((WIDE, 256), BF),
            pltpu.VMEM((WIDE, 256), BF),
            pltpu.VMEM((256, COLS), BF),
            pltpu.VMEM((NB, 3 * NB), F32),
            pltpu.VMEM((NB, NB), F32),
            pltpu.VMEM((WIDE, NB), BF),
            pltpu.VMEM((WIDE, NB), BF),
            pltpu.VMEM((NB, WIDE), BF),
            pltpu.VMEM((NB, WIDE), BF),
            pltpu.VMEM((WIDE, CELLS), F32),
        ],
        compiler_params=pltpu.CompilerParams(vmem_limit_bytes=48 * 1024 * 1024),
    )(spot, window, members, *([] if last else [obs]))


def gather_obs(value, variance, cell, field, count):
    index = field * CELLS + cell
    live = jnp.arange(CAP, dtype=jnp.int32) < count[:, None]
    columns = [index.astype(F32), value, variance, live.astype(F32), cell.astype(F32)]
    return jnp.stack(columns + [jnp.zeros_like(value)] * 3, axis=-1)


def per_device(ensemble, obs_value, obs_var, obs_cell, obs_field, obs_count):
    lines = [value.reshape(BATCHES, CAP) for value in (obs_value, obs_var, obs_cell, obs_field)]
    obs = gather_obs(*lines, obs_count.reshape(BATCHES))
    spot = jnp.stack([lax.axis_index("gy"), lax.axis_index("gx")]).astype(jnp.int32)
    members, packet = first_packet(ensemble.reshape(M * PARTS, NB), obs)
    for batch in range(BATCHES):
        window = exchange(packet).reshape(SLOTS, NB)
        if batch < BATCHES - 1:
            members, packet = analyse(spot, window, members, obs, batch)
        else:
            members = analyse(spot, window, members, obs, batch)
    return members.reshape(ensemble.shape)


def solution(mesh):
    return jax.shard_map(
        per_device,
        mesh=mesh,
        in_specs=(
            P(None, None, "gy", "gx", None),
            P(None, "gy", "gx", None),
            P(None, "gy", "gx", None),
            P(None, "gy", "gx", None),
            P(None, "gy", "gx", None),
            P(None, "gy", "gx"),
        ),
        out_specs=P(None, None, "gy", "gx", None),
        check_vma=False,
    )
```

```python
import functools
import jax
import jax.numpy as jnp
from jax import lax
from jax.experimental import pallas as pl
from jax.experimental.pallas import tpu as pltpu
from jax.sharding import PartitionSpec as P

M = 80
F = 12
TX = 16
TY = 16
CELLS = 256
CAP = 32
LOC = 16
BATCHES = 3
N_GY = 8
N_GX = 16
SLOTS = 25 * CAP
NB = 128
BLOCKS = 7
WIDE = NB * BLOCKS
COLS = F * CELLS
PARTS = COLS // NB
UNROLL = 6
STEP = 16
GROUP = 2
MESH = pl.DeviceIdType.MESH
F32 = jnp.float32
BF = jnp.bfloat16


def taper(row_a, col_a, row_b, col_b):
    down, over = row_a - row_b, col_a - col_b
    square = down * down + over * over
    inverse = lax.rsqrt(jnp.maximum(square, 1e-20))
    ratio = square * inverse * (1.0 / LOC)
    inner = (((-0.25 * ratio + 0.5) * ratio + 0.625) * ratio - 5.0 / 3.0) * ratio * ratio + 1.0
    outer = (
        ((((ratio * (1.0 / 12.0) - 0.5) * ratio + 0.625) * ratio + 5.0 / 3.0) * ratio - 5.0) * ratio
        + 4.0
        - (2.0 / 3.0 * LOC) * inverse
    )
    return jnp.where(ratio <= 1.0, inner, jnp.where(ratio < 2.0, outer, 0.0))


def split3(value):
    high = value.astype(BF)
    rest = value - high.astype(F32)
    mid = rest.astype(BF)
    low = (rest - mid.astype(F32)).astype(BF)
    return high, mid, low


def split2(value):
    high = value.astype(BF)
    return high, (value - high.astype(F32)).astype(BF)


def dot_nn(a, b, precision=None):
    return lax.dot_general(a, b, (((1,), (0,)), ((), ())), precision=precision, preferred_element_type=F32)


def dot_nt(a, b, precision=None):
    return lax.dot_general(a, b, (((1,), (1,)), ((), ())), precision=precision, preferred_element_type=F32)


def dot_tn(a, b, precision=None):
    return lax.dot_general(a, b, (((0,), (0,)), ((), ())), precision=precision, preferred_element_type=F32)


def three(dot, a, b):
    return dot(a[0], b[0]) + dot(a[1], b[0]) + dot(a[0], b[1])


def eliminate(chain, root, rows):
    lane = lax.broadcasted_iota(jnp.int32, (8, NB), 1)
    row = lax.broadcasted_iota(jnp.int32, (8, NB), 0)
    member = lane < M
    for group in range(NB // STEP // GROUP):

        @pl.when(rows > STEP * GROUP * group)
        def _():
            for k in range(GROUP * group, GROUP * group + GROUP):
                base = STEP * k
                own = STEP // 8
                ahead = own if base + STEP == NB else 2 * own
                sect = [[chain[base + 8 * h : base + 8 * h + 8, NB * s : NB * s + NB] for h in range(ahead)] for s in range(2)]
                dev = [jnp.broadcast_to(root[base + 8 * h : base + 8 * h + 8, :], (8, NB)) for h in range(own)]
                bc = [
                    [jnp.broadcast_to(sect[0][h][:, base + i : base + i + 1], (8, NB)) for h in range(ahead)]
                    for i in range(STEP)
                ]
                used = (lane >= base) & (lane < base + STEP)
                for h in range(ahead):
                    unit = jnp.where(lane == row + (base + 8 * h), 1.0, 0.0) if h < own else 0.0
                    sect[0][h] = jnp.where(used, unit, sect[0][h])
                piv = [jnp.ones((8, NB), F32) for h in range(own)]
                for j in range(STEP):
                    hj, rj = divmod(j, 8)
                    piv[hj] = jnp.where(row == rj, bc[j][hj], piv[hj])
                    pivot = jnp.broadcast_to(bc[j][hj][rj : rj + 1, :], (8, NB))
                    rs = lax.rsqrt(pivot)
                    inv = rs * rs
                    droot = jnp.broadcast_to(dev[hj][rj : rj + 1, :], (8, NB))
                    scale_y = jnp.where(member, rs / (pivot * rs + droot), inv)
                    lines = [jnp.broadcast_to(sect[s][hj][rj : rj + 1, :], (8, NB)) for s in range(2)]
                    firsts = [jnp.broadcast_to(bc[i][hj][rj : rj + 1, :], (8, NB)) for i in range(j + 1, STEP)]
                    for h in range(hj, ahead):
                        column = bc[j][h]
                        if h == hj:
                            if rj == 7:
                                continue
                            column = jnp.where(row > rj, column, 0.0)
                        mult = column * inv
                        for i in range(j + 1, STEP):
                            bc[i][h] = bc[i][h] - mult * firsts[i - j - 1]
                        sect[0][h] = sect[0][h] - mult * lines[0]
                        sect[1][h] = sect[1][h] - column * scale_y * lines[1]
                for h in range(own):
                    rs = lax.rsqrt(piv[h])
                    sect[0][h] = sect[0][h] * rs
                    sect[1][h] = sect[1][h] * jnp.where(member, 1.0 / (piv[h] * rs + dev[h]), rs)
                for h in range(ahead):
                    for s in range(2):
                        chain[base + 8 * h : base + 8 * h + 8, NB * s : NB * s + NB] = sect[s][h]
                rest = base + 2 * STEP
                if rest < NB:
                    parts = [split3(jnp.concatenate(sect[s][:own], axis=0)) for s in range(2)]
                    high, mid, low = [jnp.concatenate([parts[s][p] for s in range(2)], axis=1) for p in range(3)]
                    up, um, ul = parts[0]
                    left = jnp.concatenate([up, up, um, up, ul, um], axis=0)
                    right = jnp.concatenate([high, mid, high, low, high, mid], axis=0)
                    update = dot_tn(left, right)
                    below = lax.broadcasted_iota(jnp.int32, (NB - rest, NB), 1)
                    used = (below >= base) & (below < base + STEP)
                    chain[rest:, 0:NB] = jnp.where(used, 0.0, chain[rest:, 0:NB]) - update[rest:, 0:NB]
                    chain[rest:, NB:] = chain[rest:, NB:] - update[rest:, NB:]


def write_packet(members, obs, packet_ref):
    index = obs[:, 0:1].astype(jnp.int32)
    live = obs[:, 3:4]
    hot = (lax.broadcasted_iota(jnp.int32, (CAP, COLS), 1) == index).astype(F32).astype(BF)
    got = dot_nt(hot, jnp.concatenate(split3(members), axis=0))
    prior = got[:, 0:M] + got[:, M : 2 * M] + got[:, 2 * M :]
    mean = jnp.sum(prior, axis=1, keepdims=True) * (1.0 / M)
    perturb = jnp.concatenate([(prior - mean) * live, jnp.zeros((CAP, NB - M), F32)], axis=1)
    cell = obs[:, 4:5]
    in_row = jnp.floor(cell * (1.0 / TX))
    lane = lax.broadcasted_iota(jnp.int32, (CAP, NB), 1)
    sides = ((obs[:, 1:2] - mean) * live, obs[:, 2:3] * live, live, cell * live, in_row, cell - in_row * TX)
    for place, side in enumerate(sides):
        perturb = jnp.where(lane == M + place, side, perturb)
    packet_ref[...] = perturb


def packet_kernel(rows_ref, obs_ref, mem_ref, packet_ref):
    for part in range(PARTS):
        mem_ref[:, NB * part : NB * part + NB] = rows_ref[pl.ds(part, M, stride=PARTS), :]
    write_packet(mem_ref[...], obs_ref[0], packet_ref)


def exchange_kernel(packet_ref, win_ref, send_sem, recv_sem, own_sem):
    gy = lax.axis_index("gy")
    gx = lax.axis_index("gx")
    reach = range(-2, 3)
    row_of = {step: lax.rem(gy + step + N_GY, N_GY) for step in reach}
    col_of = {step: lax.rem(gx + step + N_GX, N_GX) for step in reach}
    others = [(down, over) for down in reach for over in reach if (down, over) != (0, 0)]
    barrier = pltpu.get_barrier_semaphore()
    for down, over in others:
        pl.semaphore_signal(barrier, inc=1, device_id=(row_of[down], col_of[over]), device_id_type=MESH)
    own = pltpu.make_async_copy(packet_ref, win_ref.at[2, 2], own_sem)
    own.start()
    own.wait()
    pl.semaphore_wait(barrier, len(others))
    copies = []
    for place, (down, over) in enumerate(others):
        copy = pltpu.make_async_remote_copy(
            src_ref=win_ref.at[2, 2],
            dst_ref=win_ref.at[2 - down, 2 - over],
            send_sem=send_sem.at[place],
            recv_sem=recv_sem.at[place],
            device_id=(row_of[down], col_of[over]),
            device_id_type=MESH,
        )
        copy.start()
        copies.append(copy)
    for copy in copies:
        copy.wait()


def analysis_kernel(spot, win_ref, mem_ref, *rest, batch):
    last = batch == BATCHES - 1
    if last:
        out_ref, *scratch = rest
    else:
        obs_ref, out_ref, packet_ref, *scratch = rest
    uh, ul, side_sys, sols, ycomp, ypack, yturn, xpack, chain, root, vh, vl, zth, ztl, rho = scratch
    scale = 1.0 / (M - 1)

    tile = lax.broadcasted_iota(jnp.int32, (32, 1), 0)
    tile_row = spot[0] + tile // 5 - 2
    tile_col = spot[1] + tile % 5 - 2
    inside = (tile_row >= 0) & (tile_row < N_GY) & (tile_col >= 0) & (tile_col < N_GX) & (tile < 25)
    counts = jnp.concatenate(
        [jnp.sum(win_ref[CAP * t : CAP * t + CAP, :], axis=0, keepdims=True) for t in range(25)]
        + [jnp.zeros((7, NB), F32)],
        axis=0,
    )[:, M + 2 : M + 3]
    counts = jnp.where(inside, counts, 0.0)
    n = jnp.sum(counts).astype(jnp.int32)
    nb = (n + NB - 1) // NB
    slot_lane = lax.broadcasted_iota(jnp.int32, (1, SLOTS), 1)
    slot_tile = slot_lane // CAP
    slot_k = (slot_lane % CAP).astype(F32)
    base = jnp.sum(jnp.where(tile < slot_tile, counts, 0.0), axis=0, keepdims=True)
    own = jnp.sum(jnp.where(tile == slot_tile, counts, 0.0), axis=0, keepdims=True)
    place = jnp.where(slot_k < own, base + slot_k, -1.0).astype(jnp.int32)

    mem = mem_ref[...]
    mean = jnp.sum(mem, axis=0, keepdims=True) * (1.0 / M)
    xh, xl = split2(mem - mean)
    xpack[0:M, :] = xh
    xpack[M : 2 * M, :] = xh
    xpack[2 * M : 3 * M, :] = xl
    xpack[3 * M :, :] = jnp.zeros((256 - 3 * M, COLS), BF)

    slot = lax.broadcasted_iota(jnp.int32, (SLOTS, NB), 0) // CAP
    slane = lax.broadcasted_iota(jnp.int32, (SLOTS, NB), 1)
    shift = jnp.where(slane == M + 4, (slot // 5 - 2) * TY, jnp.where(slane == M + 5, (slot % 5 - 2) * TX, 0))
    win = win_ref[...] + shift.astype(F32)
    win2 = jnp.concatenate(split2(win), axis=1)
    ycomp[...] = jnp.zeros_like(ycomp)
    yturn[...] = jnp.zeros_like(yturn)
    zth[...] = jnp.zeros_like(zth)
    ztl[...] = jnp.zeros_like(ztl)
    lane = lax.broadcasted_iota(jnp.int32, (NB, NB), 1)

    @pl.loop(0, nb)
    def _(b):
        at = pl.ds(pl.multiple_of(b * NB, NB), NB)
        target = lax.broadcasted_iota(jnp.int32, (NB, SLOTS), 0) + b * NB
        hot = (target == place).astype(F32).astype(BF)
        got = dot_nn(hot, win2)
        high, low = got[:, 0:NB], got[:, NB:]
        ycomp[at, :] = high + low
        high = jnp.where(lane < M, high, 0.0)
        low = jnp.where(lane < M, low, 0.0)
        turned = pltpu.roll(low, M, 1)
        ypack[at, 0:NB] = jnp.where(lane < M, high, turned).astype(BF)
        ypack[at, NB:] = jnp.where(lane < 2 * M - NB, turned, pltpu.roll(high, 2 * M - NB, 1)).astype(BF)
        turned = pltpu.roll(high, M, 1)
        yturn[at, 0:NB] = jnp.where(lane < M, high, turned).astype(BF)
        yturn[at, NB:] = jnp.where(lane < 2 * M - NB, turned, pltpu.roll(low, 2 * M - NB, 1)).astype(BF)

    side = jnp.concatenate(
        [jnp.transpose(ycomp[NB * b : NB * b + NB, :])[80:88, :] for b in range(BLOCKS)], axis=1
    )
    row_b, col_b = side[4:5, :], side[5:6, :]
    cell = lax.broadcasted_iota(jnp.int32, (1, CELLS), 1)
    cell_row = (cell // TX).astype(F32)
    cell_col = (cell % TX).astype(F32)
    srow = lax.broadcasted_iota(jnp.int32, (NB, NB), 0)

    @pl.loop(0, nb)
    def _(b):
        at = pl.ds(pl.multiple_of(b * NB, NB), NB)
        yc = ycomp[at, :]
        r_eff = yc[:, 81:82] + 1.0 - yc[:, 82:83]
        row_a, col_a = yc[:, 84:85], yc[:, 85:86]
        rho[at, :] = taper(row_a, col_a, cell_row, cell_col) * scale
        root[...] = jnp.broadcast_to(jnp.sqrt(r_eff), (NB, NB))
        left = ypack[at, :]

        for k in range(BLOCKS):

            @pl.when(b == k)
            def _():
                top = slice(0, NB * k)
                here = slice(NB * k, NB * k + NB)
                gram = dot_nt(left, yturn[NB * k :, :]) * scale
                system = taper(row_a, col_a, row_b[:, NB * k :], col_b[:, NB * k :]) * gram
                sides = jnp.where(lane <= M, yc, 0.0)
                if k:
                    update = three(dot_tn, (uh[top, here], ul[top, here]), (uh[top, NB * k :], ul[top, NB * k :]))
                    system = system - update[:, : WIDE - NB * k]
                    sides = sides - update[:, WIDE - NB * k :]
                chain[:, 0:NB] = system[:, 0:NB] + jnp.where(lane == srow, r_eff, 0.0)
                chain[:, NB:] = sides
                if k < BLOCKS - 1:
                    side_sys[:, NB * k + NB :] = system[:, NB:]

        eliminate(chain, root, n - b * NB)
        inverse = split2(jnp.where(lane <= srow, chain[:, 0:NB], 0.0))
        vh[at, :], vl[at, :] = inverse
        solved = chain[:, NB:]
        sols[at, :] = solved
        uh[at, WIDE:], ul[at, WIDE:] = split2(solved)

        for k in range(BLOCKS - 1):

            @pl.when(b == k)
            def _():
                here = slice(NB * k, NB * k + NB)
                right = slice(NB * k + NB, WIDE)
                uh[here, right], ul[here, right] = split2(three(dot_nn, inverse, split2(side_sys[:, right])))

    for k in range(BLOCKS - 1, -1, -1):

        @pl.when(k < nb)
        def _():
            here = slice(NB * k, NB * k + NB)
            target = jnp.transpose(sols[here, :])
            if k < BLOCKS - 1:
                right = slice(NB * k + NB, WIDE)
                target = target - three(dot_nt, (zth[:, right], ztl[:, right]), (uh[here, right], ul[here, right]))
            zth[:, here], ztl[:, here] = split2(three(dot_nn, split2(target), (vh[here, :], vl[here, :])))

    for used in range(1, BLOCKS + 1):

        @pl.when(nb == used)
        def _():
            here = slice(0, NB * used)
            zh = zth[0:96, here]
            both = jnp.concatenate([zh, ztl[0:96, here]], axis=0)

            def one_field(f, carry):
                at = pl.ds(pl.multiple_of(f * CELLS, CELLS), CELLS)
                gh, gl = split2(dot_nn(ypack[here, :], xpack[:, at]) * rho[here, :])
                part = dot_nn(both, gh)
                gain = part[0:96] + part[96:] + dot_nn(zh, gl)
                new = mem_ref[:, at] + gain[M : M + 1, :] - gain[0:M, :]
                if last:
                    out_ref[pl.ds(2 * f, M, stride=PARTS), :] = new[:, 0:NB]
                    out_ref[pl.ds(2 * f + 1, M, stride=PARTS), :] = new[:, NB:]
                else:
                    out_ref[:, at] = new
                return carry

            lax.fori_loop(0, F, one_field, 0, unroll=UNROLL)

    if not last:
        write_packet(out_ref[...], obs_ref[batch + 1], packet_ref)


VM = pl.BlockSpec(memory_space=pltpu.VMEM)
SM = pl.BlockSpec(memory_space=pltpu.SMEM)
PACKET = jax.ShapeDtypeStruct((CAP, NB), F32)
STATE = jax.ShapeDtypeStruct((M, COLS), F32)
ROWS = jax.ShapeDtypeStruct((M * PARTS, NB), F32)


def first_packet(rows, obs):
    return pl.pallas_call(
        packet_kernel,
        out_shape=(STATE, PACKET),
        in_specs=[VM, VM],
        out_specs=(VM, VM),
        compiler_params=pltpu.CompilerParams(vmem_limit_bytes=32 * 1024 * 1024),
    )(rows, obs)


def exchange(packet):
    return pl.pallas_call(
        exchange_kernel,
        out_shape=jax.ShapeDtypeStruct((5, 5, CAP, NB), F32),
        in_specs=[pl.BlockSpec(memory_space=pl.ANY)],
        out_specs=VM,
        scratch_shapes=[pltpu.SemaphoreType.DMA((24,)), pltpu.SemaphoreType.DMA((24,)), pltpu.SemaphoreType.DMA(())],
        compiler_params=pltpu.CompilerParams(collective_id=0, has_side_effects=True),
    )(packet)


def analyse(spot, window, members, obs, batch):
    last = batch == BATCHES - 1
    return pl.pallas_call(
        functools.partial(analysis_kernel, batch=batch),
        out_shape=ROWS if last else (STATE, PACKET),
        in_specs=[SM, VM, VM] + ([] if last else [VM]),
        out_specs=VM if last else (VM, VM),
        scratch_shapes=[
            pltpu.VMEM((WIDE, WIDE + NB), BF),
            pltpu.VMEM((WIDE, WIDE + NB), BF),
            pltpu.VMEM((NB, WIDE), F32),
            pltpu.VMEM((WIDE, NB), F32),
            pltpu.VMEM((WIDE, NB), F32),
            pltpu.VMEM((WIDE, 256), BF),
            pltpu.VMEM((WIDE, 256), BF),
            pltpu.VMEM((256, COLS), BF),
            pltpu.VMEM((NB, 2 * NB), F32),
            pltpu.VMEM((NB, NB), F32),
            pltpu.VMEM((WIDE, NB), BF),
            pltpu.VMEM((WIDE, NB), BF),
            pltpu.VMEM((NB, WIDE), BF),
            pltpu.VMEM((NB, WIDE), BF),
            pltpu.VMEM((WIDE, CELLS), F32),
        ],
        compiler_params=pltpu.CompilerParams(vmem_limit_bytes=48 * 1024 * 1024),
    )(spot, window, members, *([] if last else [obs]))


def gather_obs(value, variance, cell, field, count):
    index = field * CELLS + cell
    live = jnp.arange(CAP, dtype=jnp.int32) < count[:, None]
    columns = [index.astype(F32), value, variance, live.astype(F32), cell.astype(F32)]
    return jnp.stack(columns + [jnp.zeros_like(value)] * 3, axis=-1)


def per_device(ensemble, obs_value, obs_var, obs_cell, obs_field, obs_count):
    lines = [value.reshape(BATCHES, CAP) for value in (obs_value, obs_var, obs_cell, obs_field)]
    obs = gather_obs(*lines, obs_count.reshape(BATCHES))
    spot = jnp.stack([lax.axis_index("gy"), lax.axis_index("gx")]).astype(jnp.int32)
    members, packet = first_packet(ensemble.reshape(M * PARTS, NB), obs)
    for batch in range(BATCHES):
        window = exchange(packet).reshape(SLOTS, NB)
        if batch < BATCHES - 1:
            members, packet = analyse(spot, window, members, obs, batch)
        else:
            members = analyse(spot, window, members, obs, batch)
    return members.reshape(ensemble.shape)


def solution(mesh):
    return jax.shard_map(
        per_device,
        mesh=mesh,
        in_specs=(
            P(None, None, "gy", "gx", None),
            P(None, "gy", "gx", None),
            P(None, "gy", "gx", None),
            P(None, "gy", "gx", None),
            P(None, "gy", "gx", None),
            P(None, "gy", "gx"),
        ),
        out_specs=P(None, None, "gy", "gx", None),
        check_vma=False,
    )
```

```python
import functools
import jax
import jax.numpy as jnp
from jax import lax
from jax.experimental import pallas as pl
from jax.experimental.pallas import tpu as pltpu
from jax.sharding import PartitionSpec as P

M = 80
F = 12
TX = 16
TY = 16
CELLS = 256
CAP = 32
LOC = 16
BATCHES = 3
N_GY = 8
N_GX = 16
SLOTS = 25 * CAP
NB = 128
BLOCKS = 7
WIDE = NB * BLOCKS
COLS = F * CELLS
PARTS = COLS // NB
UNROLL = 6
STEP = 16
GROUP = 2
MESH = pl.DeviceIdType.MESH
F32 = jnp.float32
BF = jnp.bfloat16


def taper(row_a, col_a, row_b, col_b):
    down, over = row_a - row_b, col_a - col_b
    square = down * down + over * over
    inverse = lax.rsqrt(jnp.maximum(square, 1e-20))
    ratio = square * inverse * (1.0 / LOC)
    inner = (((-0.25 * ratio + 0.5) * ratio + 0.625) * ratio - 5.0 / 3.0) * ratio * ratio + 1.0
    outer = (
        ((((ratio * (1.0 / 12.0) - 0.5) * ratio + 0.625) * ratio + 5.0 / 3.0) * ratio - 5.0) * ratio
        + 4.0
        - (2.0 / 3.0 * LOC) * inverse
    )
    return jnp.where(ratio <= 1.0, inner, jnp.where(ratio < 2.0, outer, 0.0))


def split3(value):
    high = value.astype(BF)
    rest = value - high.astype(F32)
    mid = rest.astype(BF)
    low = (rest - mid.astype(F32)).astype(BF)
    return high, mid, low


def split2(value):
    high = value.astype(BF)
    return high, (value - high.astype(F32)).astype(BF)


def dot_nn(a, b, precision=None):
    return lax.dot_general(a, b, (((1,), (0,)), ((), ())), precision=precision, preferred_element_type=F32)


def dot_nt(a, b, precision=None):
    return lax.dot_general(a, b, (((1,), (1,)), ((), ())), precision=precision, preferred_element_type=F32)


def dot_tn(a, b, precision=None):
    return lax.dot_general(a, b, (((0,), (0,)), ((), ())), precision=precision, preferred_element_type=F32)


def three(dot, a, b):
    return dot(a[0], b[0]) + dot(a[1], b[0]) + dot(a[0], b[1])


def eliminate(chain, root, rows):
    lane = lax.broadcasted_iota(jnp.int32, (8, NB), 1)
    row = lax.broadcasted_iota(jnp.int32, (8, NB), 0)
    member = lane < M
    for group in range(NB // STEP // GROUP):

        @pl.when(rows > STEP * GROUP * group)
        def _():
            for k in range(GROUP * group, GROUP * group + GROUP):
                base = STEP * k
                own = STEP // 8
                ahead = own if base + STEP == NB else 2 * own
                sect = [[chain[base + 8 * h : base + 8 * h + 8, NB * s : NB * s + NB] for h in range(ahead)] for s in range(2)]
                dev = [jnp.broadcast_to(root[base + 8 * h : base + 8 * h + 8, :], (8, NB)) for h in range(own)]
                bc = [
                    [jnp.broadcast_to(sect[0][h][:, base + i : base + i + 1], (8, NB)) for h in range(ahead)]
                    for i in range(STEP)
                ]
                used = (lane >= base) & (lane < base + STEP)
                for h in range(ahead):
                    unit = jnp.where(lane == row + (base + 8 * h), 1.0, 0.0) if h < own else 0.0
                    sect[0][h] = jnp.where(used, unit, sect[0][h])
                piv = [jnp.ones((8, NB), F32) for h in range(own)]
                for j in range(STEP):
                    hj, rj = divmod(j, 8)
                    piv[hj] = jnp.where(row == rj, bc[j][hj], piv[hj])
                    pivot = jnp.broadcast_to(bc[j][hj][rj : rj + 1, :], (8, NB))
                    rs = lax.rsqrt(pivot)
                    inv = rs * rs
                    droot = jnp.broadcast_to(dev[hj][rj : rj + 1, :], (8, NB))
                    scale_y = jnp.where(member, rs / (pivot * rs + droot), inv)
                    lines = [jnp.broadcast_to(sect[s][hj][rj : rj + 1, :], (8, NB)) for s in range(2)]
                    firsts = [jnp.broadcast_to(bc[i][hj][rj : rj + 1, :], (8, NB)) for i in range(j + 1, STEP)]
                    for h in range(hj, ahead):
                        column = bc[j][h]
                        if h == hj:
                            if rj == 7:
                                continue
                            column = jnp.where(row > rj, column, 0.0)
                        mult = column * inv
                        for i in range(j + 1, STEP):
                            bc[i][h] = bc[i][h] - mult * firsts[i - j - 1]
                        sect[0][h] = sect[0][h] - mult * lines[0]
                        sect[1][h] = sect[1][h] - column * scale_y * lines[1]
                for h in range(own):
                    rs = lax.rsqrt(piv[h])
                    sect[0][h] = sect[0][h] * rs
                    sect[1][h] = sect[1][h] * jnp.where(member, 1.0 / (piv[h] * rs + dev[h]), rs)
                for h in range(ahead):
                    for s in range(2):
                        chain[base + 8 * h : base + 8 * h + 8, NB * s : NB * s + NB] = sect[s][h]
                rest = base + 2 * STEP
                if rest < NB:
                    parts = [split3(jnp.concatenate(sect[s][:own], axis=0)) for s in range(2)]
                    high, mid, low = [jnp.concatenate([parts[s][p] for s in range(2)], axis=1) for p in range(3)]
                    up, um, ul = parts[0]
                    left = jnp.concatenate([up, up, um, up, ul, um], axis=0)
                    right = jnp.concatenate([high, mid, high, low, high, mid], axis=0)
                    update = dot_tn(left, right)
                    below = lax.broadcasted_iota(jnp.int32, (NB - rest, NB), 1)
                    used = (below >= base) & (below < base + STEP)
                    chain[rest:, 0:NB] = jnp.where(used, 0.0, chain[rest:, 0:NB]) - update[rest:, 0:NB]
                    chain[rest:, NB:] = chain[rest:, NB:] - update[rest:, NB:]


def write_packet(members, obs, packet_ref):
    index = obs[:, 0:1].astype(jnp.int32)
    live = obs[:, 3:4]
    hot = (lax.broadcasted_iota(jnp.int32, (CAP, COLS), 1) == index).astype(F32).astype(BF)
    got = dot_nt(hot, jnp.concatenate(split3(members), axis=0))
    prior = got[:, 0:M] + got[:, M : 2 * M] + got[:, 2 * M :]
    mean = jnp.sum(prior, axis=1, keepdims=True) * (1.0 / M)
    perturb = jnp.concatenate([(prior - mean) * live, jnp.zeros((CAP, NB - M), F32)], axis=1)
    cell = obs[:, 4:5]
    in_row = jnp.floor(cell * (1.0 / TX))
    lane = lax.broadcasted_iota(jnp.int32, (CAP, NB), 1)
    sides = ((obs[:, 1:2] - mean) * live, obs[:, 2:3] * live, live, cell * live, in_row, cell - in_row * TX)
    for place, side in enumerate(sides):
        perturb = jnp.where(lane == M + place, side, perturb)
    packet_ref[...] = perturb


def packet_kernel(rows_ref, obs_ref, mem_ref, packet_ref):
    for part in range(PARTS):
        mem_ref[:, NB * part : NB * part + NB] = rows_ref[pl.ds(part, M, stride=PARTS), :]
    write_packet(mem_ref[...], obs_ref[0], packet_ref)


def exchange_kernel(packet_ref, win_ref, send_sem, recv_sem, own_sem):
    gy = lax.axis_index("gy")
    gx = lax.axis_index("gx")
    reach = range(-2, 3)
    row_of = {step: lax.rem(gy + step + N_GY, N_GY) for step in reach}
    col_of = {step: lax.rem(gx + step + N_GX, N_GX) for step in reach}
    others = [(down, over) for down in reach for over in reach if (down, over) != (0, 0)]
    barrier = pltpu.get_barrier_semaphore()
    for down, over in others:
        pl.semaphore_signal(barrier, inc=1, device_id=(row_of[down], col_of[over]), device_id_type=MESH)
    own = pltpu.make_async_copy(packet_ref, win_ref.at[2, 2], own_sem)
    own.start()
    own.wait()
    pl.semaphore_wait(barrier, len(others))
    copies = []
    for place, (down, over) in enumerate(others):
        copy = pltpu.make_async_remote_copy(
            src_ref=win_ref.at[2, 2],
            dst_ref=win_ref.at[2 - down, 2 - over],
            send_sem=send_sem.at[place],
            recv_sem=recv_sem.at[place],
            device_id=(row_of[down], col_of[over]),
            device_id_type=MESH,
        )
        copy.start()
        copies.append(copy)
    for copy in copies:
        copy.wait()


def analysis_kernel(spot, win_ref, mem_ref, *rest, batch):
    last = batch == BATCHES - 1
    if last:
        out_ref, *scratch = rest
    else:
        obs_ref, out_ref, packet_ref, *scratch = rest
    uh, ul, side_sys, sols, ycomp, ypack, yturn, xpack, chain, root, vh, vl, zth, ztl, rho = scratch
    scale = 1.0 / (M - 1)

    tile = lax.broadcasted_iota(jnp.int32, (32, 1), 0)
    tile_row = spot[0] + tile // 5 - 2
    tile_col = spot[1] + tile % 5 - 2
    inside = (tile_row >= 0) & (tile_row < N_GY) & (tile_col >= 0) & (tile_col < N_GX) & (tile < 25)
    counts = jnp.concatenate(
        [jnp.sum(win_ref[CAP * t : CAP * t + CAP, :], axis=0, keepdims=True) for t in range(25)]
        + [jnp.zeros((7, NB), F32)],
        axis=0,
    )[:, M + 2 : M + 3]
    counts = jnp.where(inside, counts, 0.0)
    n = jnp.sum(counts).astype(jnp.int32)
    nb = (n + NB - 1) // NB
    slot_lane = lax.broadcasted_iota(jnp.int32, (1, SLOTS), 1)
    slot_tile = slot_lane // CAP
    slot_k = (slot_lane % CAP).astype(F32)
    base = jnp.sum(jnp.where(tile < slot_tile, counts, 0.0), axis=0, keepdims=True)
    own = jnp.sum(jnp.where(tile == slot_tile, counts, 0.0), axis=0, keepdims=True)
    place = jnp.where(slot_k < own, base + slot_k, -1.0).astype(jnp.int32)

    mem = mem_ref[...]
    mean = jnp.sum(mem, axis=0, keepdims=True) * (1.0 / M)
    xh, xl = split2(mem - mean)
    xpack[0:M, :] = xh
    xpack[M : 2 * M, :] = xh
    xpack[2 * M : 3 * M, :] = xl
    xpack[3 * M :, :] = jnp.zeros((256 - 3 * M, COLS), BF)

    slot = lax.broadcasted_iota(jnp.int32, (SLOTS, NB), 0) // CAP
    slane = lax.broadcasted_iota(jnp.int32, (SLOTS, NB), 1)
    shift = jnp.where(slane == M + 4, (slot // 5 - 2) * TY, jnp.where(slane == M + 5, (slot % 5 - 2) * TX, 0))
    win = win_ref[...] + shift.astype(F32)
    win2 = jnp.concatenate(split2(win), axis=1)
    ycomp[...] = jnp.zeros_like(ycomp)
    yturn[...] = jnp.zeros_like(yturn)
    zth[...] = jnp.zeros_like(zth)
    ztl[...] = jnp.zeros_like(ztl)
    lane = lax.broadcasted_iota(jnp.int32, (NB, NB), 1)

    @pl.loop(0, nb)
    def _(b):
        at = pl.ds(pl.multiple_of(b * NB, NB), NB)
        target = lax.broadcasted_iota(jnp.int32, (NB, SLOTS), 0) + b * NB
        hot = (target == place).astype(F32).astype(BF)
        got = dot_nn(hot, win2)
        high, low = got[:, 0:NB], got[:, NB:]
        ycomp[at, :] = high + low
        high = jnp.where(lane < M, high, 0.0)
        low = jnp.where(lane < M, low, 0.0)
        turned = pltpu.roll(low, M, 1)
        ypack[at, 0:NB] = jnp.where(lane < M, high, turned).astype(BF)
        ypack[at, NB:] = jnp.where(lane < 2 * M - NB, turned, pltpu.roll(high, 2 * M - NB, 1)).astype(BF)
        turned = pltpu.roll(high, M, 1)
        yturn[at, 0:NB] = jnp.where(lane < M, high, turned).astype(BF)
        yturn[at, NB:] = jnp.where(lane < 2 * M - NB, turned, pltpu.roll(low, 2 * M - NB, 1)).astype(BF)

    side = jnp.concatenate(
        [jnp.transpose(ycomp[NB * b : NB * b + NB, :])[80:88, :] for b in range(BLOCKS)], axis=1
    )
    row_b, col_b = side[4:5, :], side[5:6, :]
    cell = lax.broadcasted_iota(jnp.int32, (1, CELLS), 1)
    cell_row = (cell // TX).astype(F32)
    cell_col = (cell % TX).astype(F32)
    srow = lax.broadcasted_iota(jnp.int32, (NB, NB), 0)

    @pl.loop(0, nb)
    def _(b):
        at = pl.ds(pl.multiple_of(b * NB, NB), NB)
        yc = ycomp[at, :]
        r_eff = yc[:, 81:82] + 1.0 - yc[:, 82:83]
        row_a, col_a = yc[:, 84:85], yc[:, 85:86]
        rho[at, :] = taper(row_a, col_a, cell_row, cell_col) * scale
        root[...] = jnp.broadcast_to(jnp.sqrt(r_eff), (NB, NB))
        left = ypack[at, :]

        for k in range(BLOCKS):

            @pl.when(b == k)
            def _():
                top = slice(0, NB * k)
                here = slice(NB * k, NB * k + NB)
                gram = dot_nt(left, yturn[NB * k :, :]) * scale
                system = taper(row_a, col_a, row_b[:, NB * k :], col_b[:, NB * k :]) * gram
                sides = jnp.where(lane <= M, yc, 0.0)
                if k:
                    update = three(dot_tn, (uh[top, here], ul[top, here]), (uh[top, NB * k :], ul[top, NB * k :]))
                    system = system - update[:, : WIDE - NB * k]
                    sides = sides - update[:, WIDE - NB * k :]
                chain[:, 0:NB] = system[:, 0:NB] + jnp.where(lane == srow, r_eff, 0.0)
                chain[:, NB:] = sides
                if k < BLOCKS - 1:
                    side_sys[:, NB * k + NB :] = system[:, NB:]

        eliminate(chain, root, n - b * NB)
        inverse = split2(jnp.where(lane <= srow, chain[:, 0:NB], 0.0))
        vh[at, :], vl[at, :] = inverse
        solved = chain[:, NB:]
        sols[at, :] = solved
        uh[at, WIDE:], ul[at, WIDE:] = split2(solved)

        for k in range(BLOCKS - 1):

            @pl.when(b == k)
            def _():
                here = slice(NB * k, NB * k + NB)
                right = slice(NB * k + NB, WIDE)
                uh[here, right], ul[here, right] = split2(three(dot_nn, inverse, split2(side_sys[:, right])))

    for k in range(BLOCKS - 1, -1, -1):

        @pl.when(k < nb)
        def _():
            here = slice(NB * k, NB * k + NB)
            target = jnp.transpose(sols[here, :])
            if k < BLOCKS - 1:
                right = slice(NB * k + NB, WIDE)
                target = target - three(dot_nt, (zth[:, right], ztl[:, right]), (uh[here, right], ul[here, right]))
            zth[:, here], ztl[:, here] = split2(three(dot_nn, split2(target), (vh[here, :], vl[here, :])))

    for used in range(1, BLOCKS + 1):

        @pl.when(nb == used)
        def _():
            here = slice(0, NB * used)
            zh = zth[0:96, here]
            both = jnp.concatenate([zh, ztl[0:96, here]], axis=0)

            def one_field(f, carry):
                at = pl.ds(pl.multiple_of(f * CELLS, CELLS), CELLS)
                gh, gl = split2(dot_nn(ypack[here, :], xpack[:, at]) * rho[here, :])
                part = dot_nn(both, gh)
                gain = part[0:96] + part[96:] + dot_nn(zh, gl)
                new = mem_ref[:, at] + gain[M : M + 1, :] - gain[0:M, :]
                if last:
                    out_ref[pl.ds(2 * f, M, stride=PARTS), :] = new[:, 0:NB]
                    out_ref[pl.ds(2 * f + 1, M, stride=PARTS), :] = new[:, NB:]
                else:
                    out_ref[:, at] = new
                return carry

            lax.fori_loop(0, F, one_field, 0, unroll=UNROLL)

    if not last:
        write_packet(out_ref[...], obs_ref[batch + 1], packet_ref)


VM = pl.BlockSpec(memory_space=pltpu.VMEM)
SM = pl.BlockSpec(memory_space=pltpu.SMEM)
PACKET = jax.ShapeDtypeStruct((CAP, NB), F32)
STATE = jax.ShapeDtypeStruct((M, COLS), F32)
ROWS = jax.ShapeDtypeStruct((M * PARTS, NB), F32)


def first_packet(rows, obs):
    return pl.pallas_call(
        packet_kernel,
        out_shape=(STATE, PACKET),
        in_specs=[VM, VM],
        out_specs=(VM, VM),
        compiler_params=pltpu.CompilerParams(vmem_limit_bytes=32 * 1024 * 1024),
    )(rows, obs)


def exchange(packet):
    return pl.pallas_call(
        exchange_kernel,
        out_shape=jax.ShapeDtypeStruct((5, 5, CAP, NB), F32),
        in_specs=[pl.BlockSpec(memory_space=pl.ANY)],
        out_specs=VM,
        scratch_shapes=[pltpu.SemaphoreType.DMA((24,)), pltpu.SemaphoreType.DMA((24,)), pltpu.SemaphoreType.DMA(())],
        compiler_params=pltpu.CompilerParams(
            collective_id=0, has_side_effects=True, vmem_limit_bytes=4 * 1024 * 1024
        ),
    )(packet)


def analyse(spot, window, members, obs, batch):
    last = batch == BATCHES - 1
    return pl.pallas_call(
        functools.partial(analysis_kernel, batch=batch),
        out_shape=ROWS if last else (STATE, PACKET),
        in_specs=[SM, VM, VM] + ([] if last else [VM]),
        out_specs=VM if last else (VM, VM),
        scratch_shapes=[
            pltpu.VMEM((WIDE, WIDE + NB), BF),
            pltpu.VMEM((WIDE, WIDE + NB), BF),
            pltpu.VMEM((NB, WIDE), F32),
            pltpu.VMEM((WIDE, NB), F32),
            pltpu.VMEM((WIDE, NB), F32),
            pltpu.VMEM((WIDE, 256), BF),
            pltpu.VMEM((WIDE, 256), BF),
            pltpu.VMEM((256, COLS), BF),
            pltpu.VMEM((NB, 2 * NB), F32),
            pltpu.VMEM((NB, NB), F32),
            pltpu.VMEM((WIDE, NB), BF),
            pltpu.VMEM((WIDE, NB), BF),
            pltpu.VMEM((NB, WIDE), BF),
            pltpu.VMEM((NB, WIDE), BF),
            pltpu.VMEM((WIDE, CELLS), F32),
        ],
        compiler_params=pltpu.CompilerParams(vmem_limit_bytes=48 * 1024 * 1024),
    )(spot, window, members, *([] if last else [obs]))


def gather_obs(value, variance, cell, field, count):
    index = field * CELLS + cell
    live = jnp.arange(CAP, dtype=jnp.int32) < count[:, None]
    columns = [index.astype(F32), value, variance, live.astype(F32), cell.astype(F32)]
    return jnp.stack(columns + [jnp.zeros_like(value)] * 3, axis=-1)


def per_device(ensemble, obs_value, obs_var, obs_cell, obs_field, obs_count):
    lines = [value.reshape(BATCHES, CAP) for value in (obs_value, obs_var, obs_cell, obs_field)]
    obs = gather_obs(*lines, obs_count.reshape(BATCHES))
    spot = jnp.stack([lax.axis_index("gy"), lax.axis_index("gx")]).astype(jnp.int32)
    members, packet = first_packet(ensemble.reshape(M * PARTS, NB), obs)
    for batch in range(BATCHES):
        window = exchange(packet).reshape(SLOTS, NB)
        if batch < BATCHES - 1:
            members, packet = analyse(spot, window, members, obs, batch)
        else:
            members = analyse(spot, window, members, obs, batch)
    return members.reshape(ensemble.shape)


def solution(mesh):
    return jax.shard_map(
        per_device,
        mesh=mesh,
        in_specs=(
            P(None, None, "gy", "gx", None),
            P(None, "gy", "gx", None),
            P(None, "gy", "gx", None),
            P(None, "gy", "gx", None),
            P(None, "gy", "gx", None),
            P(None, "gy", "gx"),
        ),
        out_specs=P(None, None, "gy", "gx", None),
        check_vma=False,
    )
```
